512 devices in a mesh: ctx: 128 (over x, z_hi, y, core), kvh: 4 (over z_lo).
Axes of the slice: x: 4, y: 8, z: 8 (z_hi: 2, z_lo: 4; z = z_hi * 4 + z_lo), core: 2. Of those that a mesh axis runs over, the one named last changes fastest.
Arguments:
- queries: bfloat16 [16384, 2048], P('ctx', 'kvh'), parts along dimension 1, may hold values from -56 to 56
- keys: bfloat16 [16384, 512], P('ctx', 'kvh'), parts along dimension 1, may hold values from -4 to 4
- values: bfloat16 [16384, 512], P('ctx', 'kvh'), parts along dimension 1, may hold values from -6 to 6
- segment_ids: int32 [16384], P('ctx'), may hold values from 0 to 15, never falling along the last dimension, each value on 1 to 8320 neighbouring positions
Outputs:
- attended: bfloat16 [16384, 2048], P('ctx', 'kvh'), parts along dimension 1
The draws below stay inside these ranges and needn't reach their ends.
There are 4 independent parts, one for each index of `kvh`. The reference program is written for one: setup_inputs(seed, part) draws one part's arguments, and reference() takes and returns one part's arrays. A program takes and returns all parts, laid end to end along the dimension named above; an argument that names none is the same for every part. Nothing has to cross between parts.
All inputs are finite; a program needn't handle non-finite values.
Results may differ from the reference program's by a relative error of at most 0.0045.
Values may be sent and summed in bfloat16 or wider, within the bound.
A program may use at most 128 MiB of HBM per device.

```python
import math
import jax
import jax.numpy as jnp
import numpy as np
from jax import lax

HQ = 4
HD = 128
TOKENS = 16384
DOCS = 16
DOC_MOST = 8320


def shared_base(key):
    return jnp.clip(jax.random.normal(key, (TOKENS, HD), jnp.float32), -4.0, 4.0)


def draw_keys(key, part):
    base = shared_base(key)
    return base.astype(jnp.bfloat16)


def draw_queries(key, part):
    key = jax.random.fold_in(key, 7)
    fresh = jnp.clip(jax.random.normal(key, (TOKENS, HQ, HD), jnp.float32), -4.0, 4.0)
    return fresh.reshape(TOKENS, HQ * HD).astype(jnp.bfloat16)


def shard_levels(rng, shape, cuts, low, top_value):
    gain = 1.0
    for position, shards_of in cuts:
        heights = jax.random.uniform(jax.random.fold_in(jax.random.fold_in(rng, 6), position), (shards_of,), jnp.float32, low / len(cuts), top_value / len(cuts))
        gain = gain * jnp.repeat(jnp.exp(heights), shape[position] // shards_of).reshape((-1,) + (1,) * (len(shape) - 1 - position))
    return gain


def split_up(number_of, total, reach, lean):
    loads = [(1 << 20) // math.isqrt(grade ** lean) + 1 for grade in range(2, number_of + 1)]
    surplus, given = total - reach - (number_of - 1), [1] * (number_of - 1)
    while surplus > 0:
        free = [i for i in range(number_of - 1) if given[i] < reach]
        whole, budget = sum([loads[i] for i in free]), surplus
        for i in free:
            addition = min(reach - given[i], max(1, budget * loads[i] // whole), surplus)
            given[i] = given[i] + addition
            surplus = surplus - addition
    return np.array([reach] + given)


def uneven_parts(rng, number_of, total, bound, lean):
    if number_of == 2:
        one = jax.random.randint(rng, (), max(1, total - bound), min(bound, total - 1) + 1)
        return jnp.stack([one, total - one])
    tallies = jnp.asarray(split_up(number_of, total, bound, lean), jnp.int32)
    pairs = (number_of - 1) // 2
    source_of, receiver = tallies[1:1 + 2 * pairs:2], tallies[2:2 + 2 * pairs:2]
    room = jnp.minimum(source_of - 1, bound - receiver)
    passed = jax.random.randint(jax.random.fold_in(rng, 1), (pairs,), 0, 1 << 20) % (room + 1)
    tallies = tallies.at[1:1 + 2 * pairs:2].set(source_of - passed).at[2:2 + 2 * pairs:2].set(receiver + passed)
    return tallies[jax.random.permutation(jax.random.fold_in(rng, 2), number_of)]


def centred(key, extent, scale, reach, split=(), held_as=jnp.bfloat16):
    level = shard_levels(key, extent, split, -0.22, 0.18) if split else 1.0
    entries = jax.random.normal(key, extent, jnp.float32) * scale * level
    return jnp.minimum(jnp.maximum(entries, -reach), reach).astype(held_as)


def setup_inputs(seed: int = 0, part: int = 0) -> dict:
    seeds = jax.random.split(jax.random.key(seed), 5)
    part_splits = jax.random.split(jax.random.fold_in(seeds[4], part), 5)
    return {
        "queries": draw_queries(jax.random.fold_in(jax.random.fold_in(seeds[4], part), 71), part),
        "keys": draw_keys(jax.random.fold_in(jax.random.fold_in(seeds[4], part), 71), part),
        "values": centred(part_splits[2], (TOKENS, HD), 1.0, 6.0, ((0, 128),)),
        "segment_ids": jnp.searchsorted(jnp.cumsum(uneven_parts(seeds[3], DOCS, TOKENS, DOC_MOST, 2)), jnp.arange(TOKENS), side="right").astype(jnp.int32),
    }


def reference(queries, keys, values, segment_ids):
    tokens = queries.shape[0]
    head_dim = keys.shape[1]
    heads = queries.shape[1] // head_dim
    block = 128
    scale = head_dim ** -0.5
    key_pos = jnp.arange(tokens, dtype=jnp.int32)
    keys_wide = keys.astype(jnp.float32)
    values_wide = values.astype(jnp.float32)

    def one_block(index):
        start = (index * block).astype(jnp.int32)
        query_rows = lax.dynamic_slice_in_dim(queries, start, block, 0)
        query_rows = query_rows.reshape(block, heads, head_dim).astype(jnp.float32)
        query_seg = lax.dynamic_slice_in_dim(segment_ids, start, block, 0)
        query_pos = start + jnp.arange(block, dtype=jnp.int32)
        score = jnp.einsum("thd,nd->thn", query_rows, keys_wide) * scale
        allowed = (key_pos[None, :] <= query_pos[:, None]) & (segment_ids[None, :] == query_seg[:, None])
        masked = jnp.where(allowed[:, None, :], score, -1e30)
        top = jnp.max(masked, axis=2, keepdims=True)
        weight = jnp.where(allowed[:, None, :], jnp.exp(masked - top), 0.0)
        total = jnp.sum(weight, axis=2)
        rounded = lax.optimization_barrier(weight.astype(jnp.bfloat16))
        summed = jnp.einsum("thn,nd->thd", rounded.astype(jnp.float32), values_wide)
        result = summed / total[:, :, None]
        return result.reshape(block, heads * head_dim).astype(jnp.bfloat16)

    blocks = lax.map(one_block, jnp.arange(tokens // block, dtype=jnp.int32))
    return blocks.reshape(tokens, heads * head_dim)
```

```python
import functools
import math

import jax
import jax.numpy as jnp
from jax import lax
from jax.experimental import pallas as pl
from jax.experimental.pallas import tpu as pltpu
from jax.sharding import PartitionSpec as P

MESH = pl.DeviceIdType.MESH
RING = 8
BLOCKS = 2 * RING
RINGS = 8
REACH = 4
TOK = 128
HEAD = 128
HEADS = 4
ROWS = 272
LOW = -2e30
ITEMS = REACH + 1


def kernel(
    q_ref, k_ref, v_ref, seg_ref, o_ref,
    kv, edge, qseg, top, total, summed,
    xz_send, xz_recv, y_send, y_recv, c_send, c_recv, e_send, e_recv,
):
    me = lax.axis_index("ctx")
    off = lax.rem(me, BLOCKS)
    ring = me // BLOCKS
    c = lax.rem(me, 2)
    y = off // 2
    unit_scale = HEAD**-0.5 * math.log2(math.e)

    def at(dy):
        return 2 * lax.rem(y + dy + RING, RING) + c

    up = ring * BLOCKS + at(1)
    down = ring * BLOCKS + at(-1)
    twin = me + 1 - 2 * c

    def remote(src, dst, send, recv, to):
        return pltpu.make_async_remote_copy(
            src_ref=src, dst_ref=dst, send_sem=send, recv_sem=recv,
            device_id={"ctx": to}, device_id_type=MESH,
        )

    has_edge = (off == 0) & (ring >= ITEMS)
    gives_edge = (off == BLOCKS - 1) & (ring + ITEMS < RINGS)

    barrier = pltpu.get_barrier_semaphore()
    for to in (up, down, twin):
        pl.semaphore_signal(barrier, inc=1, device_id={"ctx": to}, device_id_type=MESH)
    for d in range(1, ITEMS):

        @pl.when(ring >= d)
        def _():
            pl.semaphore_signal(
                barrier, inc=1, device_id={"ctx": me - d * BLOCKS}, device_id_type=MESH
            )

    @pl.when(has_edge)
    def _():
        pl.semaphore_signal(
            barrier, inc=1, device_id={"ctx": me - REACH * BLOCKS - 1}, device_id_type=MESH
        )

    kv[0, off, pl.ds(0, TOK), :] = k_ref[...]
    kv[0, off, pl.ds(TOK, TOK), :] = v_ref[...]
    seg_row = seg_ref[...].astype(jnp.float32)
    kv[0, off, pl.ds(2 * TOK, 16), :] = jnp.broadcast_to(seg_row, (16, TOK)).astype(jnp.bfloat16)
    qseg[...] = jnp.broadcast_to(seg_row, (TOK, TOK)).T
    top[...] = jnp.full(top.shape, -1e30, jnp.float32)
    total[...] = jnp.zeros_like(total)
    summed[...] = jnp.zeros_like(summed)

    pl.semaphore_wait(
        barrier, 3 + jnp.minimum(RINGS - 1 - ring, REACH) + gives_edge.astype(jnp.int32)
    )

    def delta(k):
        return lax.rem(2 * k, ITEMS)

    def xz(k, to):
        return remote(
            kv.at[0, off], kv.at[k, off], xz_send.at[k], xz_recv.at[k], to
        )

    def hop(k, dy, slot, to):
        b = at(dy)
        return remote(kv.at[k, b], kv.at[k, b], y_send.at[k, slot], y_recv.at[k, slot], to)

    def cross(k, dy, slot):
        b = at(dy)
        return remote(kv.at[k, b], kv.at[k, b], c_send.at[k, slot], c_recv.at[k, slot], twin)

    def cross_in(k, dy, slot):
        b = 2 * lax.rem(y + dy + RING, RING) + 1 - c
        return remote(kv.at[k, b], kv.at[k, b], c_send.at[k, slot], c_recv.at[k, slot], twin)

    def launch(k):
        hop(k, 0, 1, up).start()
        hop(k, 0, 4, down).start()
        cross(k, 0, 0).start()

    launch(0)
    for k in (3, 4, 1, 2):
        d = 2 * k % ITEMS

        @pl.when(ring + d < RINGS)
        def _():
            xz(k, me + d * BLOCKS).start()

    def edge_copy(to):
        return remote(kv.at[0, off], edge, e_send, e_recv, to)

    @pl.when(gives_edge)
    def _():
        edge_copy(me + REACH * BLOCKS + 1).start()

    def arrive(k, h):
        if h < 4:
            hop(k, -h, h, up).wait_recv()
            if h < 3:
                hop(k, -h, h + 1, up).start()
            else:

                @pl.when(c == 0)
                def _():
                    hop(k, -3, 7, up).start()

            cross(k, -h, h).start()
            hop(k, h, 3 + h, down).wait_recv()
            if h < 3:
                hop(k, h, 4 + h, down).start()
            else:

                @pl.when(c == 1)
                def _():
                    hop(k, 3, 7, down).start()

            cross(k, h, 3 + h).start()
        else:
            hop(k, 4, 7, up).wait_recv()
            cross(k, 4, 7).start()

    lane = lax.broadcasted_iota(jnp.int32, (TOK, TOK), 1)
    row = lax.broadcasted_iota(jnp.int32, (TOK, TOK), 0)
    gap = row - lane

    def fold(blocks, ahead):
        keys = jnp.concatenate([b[pl.ds(0, TOK), :] for b in blocks], axis=0)
        values = jnp.concatenate([b[pl.ds(TOK, TOK), :] for b in blocks], axis=0)
        allowed = []
        for b, a in zip(blocks, ahead):
            seg = b[pl.ds(2 * TOK, 16), :].astype(jnp.float32)[0:1, :]
            allowed.append((seg == qseg[...]) & (gap >= a))
        for h in range(HEADS):
            score = lax.dot_general(
                q_ref[:, h * HEAD : (h + 1) * HEAD], keys, (((1,), (1,)), ((), ())),
                preferred_element_type=jnp.float32,
            )
            parts = [
                jnp.where(allowed[n], score[:, n * TOK : (n + 1) * TOK] * unit_scale, LOW)
                for n in range(len(blocks))
            ]
            old = top[h]
            most = functools.reduce(jnp.maximum, parts)
            new = jnp.maximum(old, jnp.max(most, axis=1, keepdims=True))
            keep = jnp.exp2(old - new)
            weights = [jnp.exp2(p - new) for p in parts]
            top[h] = new
            total[h] = total[h] * keep + functools.reduce(jnp.add, weights)
            rounded = jnp.concatenate([w.astype(jnp.bfloat16) for w in weights], axis=1)
            summed[h] = summed[h] * keep + jnp.dot(
                rounded, values, preferred_element_type=jnp.float32
            )

    def unit(k, h):
        if h < 4:
            cross_in(k, -h, h).wait_recv()
            cross_in(k, h, 3 + h).wait_recv()
            first = (-h, h)
        else:
            cross_in(k, 0, 0).wait_recv()
            cross_in(k, 4, 7).wait_recv()
            first = (0, 4)
        blocks, ahead = [], []
        for dy in first:
            chip = lax.rem(y + dy + RING, RING)
            for core in range(2):
                b = 2 * chip + core
                blocks.append(kv.at[k, b])
                ahead.append((b - off - delta(k) * BLOCKS) * TOK)
        fold(blocks, ahead)

    def drain(k):
        for slot in range(1, 7):
            hop(k, 0, slot, up).wait_send()
        hop(k, 0, 7, up).wait_send()
        for slot in range(8):
            cross(k, 0, slot).wait_send()

    def here(k):
        return (k >= 0) & (k < ITEMS) & (ring >= delta(jnp.maximum(k, 0)))

    def step(j, _):
        @pl.when(here(j - 1))
        def _():
            arrive(j - 1, 3)

        @pl.when(here(j))
        def _():
            arrive(j, 1)

        @pl.when(here(j - 2))
        def _():
            unit(j - 2, 4)

        @pl.when(here(j - 1))
        def _():
            unit(j - 1, 2)

        @pl.when(here(j - 1))
        def _():
            arrive(j - 1, 4)

        @pl.when(here(j))
        def _():
            arrive(j, 2)

        @pl.when(here(j + 1))
        def _():
            xz(j + 1, me).wait_recv()
            launch(j + 1)

        @pl.when(here(j - 1))
        def _():
            unit(j - 1, 3)

        @pl.when(here(j))
        def _():
            unit(j, 1)

        @pl.when(here(j - 2))
        def _():
            drain(j - 2)

        @pl.when(has_edge & (j == 4))
        def _():
            edge_copy(me).wait_recv()
            fold([edge], [jnp.int32(-ITEMS * BLOCKS * TOK + (BLOCKS - 1) * TOK)])

        return 0

    lax.fori_loop(0, ITEMS + 2, step, 0)

    for h in range(HEADS):
        whole = jnp.sum(total[h], axis=1, keepdims=True)
        o_ref[:, h * HEAD : (h + 1) * HEAD] = (summed[h] / whole).astype(jnp.bfloat16)

    for k in range(1, ITEMS):
        d = 2 * k % ITEMS

        @pl.when(ring + d < RINGS)
        def _():
            xz(k, me).wait_send()

    @pl.when(gives_edge)
    def _():
        edge_copy(me).wait_send()


def body(queries, keys, values, segment_ids):
    vmem = pl.BlockSpec(memory_space=pltpu.VMEM)
    return pl.pallas_call(
        kernel,
        out_shape=jax.ShapeDtypeStruct(queries.shape, queries.dtype),
        in_specs=[vmem] * 4,
        out_specs=vmem,
        scratch_shapes=[
            pltpu.VMEM((ITEMS, BLOCKS, ROWS, HEAD), jnp.bfloat16),
            pltpu.VMEM((ROWS, HEAD), jnp.bfloat16),
            pltpu.VMEM((TOK, TOK), jnp.float32),
            pltpu.VMEM((HEADS, TOK, HEAD), jnp.float32),
            pltpu.VMEM((HEADS, TOK, HEAD), jnp.float32),
            pltpu.VMEM((HEADS, TOK, HEAD), jnp.float32),
            pltpu.SemaphoreType.DMA((ITEMS,)),
            pltpu.SemaphoreType.DMA((ITEMS,)),
            pltpu.SemaphoreType.DMA((ITEMS, 8)),
            pltpu.SemaphoreType.DMA((ITEMS, 8)),
            pltpu.SemaphoreType.DMA((ITEMS, 8)),
            pltpu.SemaphoreType.DMA((ITEMS, 8)),
            pltpu.SemaphoreType.DMA,
            pltpu.SemaphoreType.DMA,
        ],
        compiler_params=pltpu.CompilerParams(
            collective_id=0, has_side_effects=True, vmem_limit_bytes=40 << 20
        ),
        name="attend_ring",
    )(queries, keys, values, segment_ids.reshape(1, TOK))


def solution(mesh):
    return jax.shard_map(
        body,
        mesh=mesh,
        in_specs=(P("ctx", "kvh"), P("ctx", "kvh"), P("ctx", "kvh"), P("ctx")),
        out_specs=P("ctx", "kvh"),
        check_vma=False,
    )
```

```python
import functools
import math

import jax
import jax.numpy as jnp
from jax import lax
from jax.experimental import pallas as pl
from jax.experimental.pallas import tpu as pltpu
from jax.sharding import PartitionSpec as P

MESH = pl.DeviceIdType.MESH
RING = 8
BLOCKS = 2 * RING
RINGS = 8
REACH = 4
TOK = 128
HEAD = 128
HEADS = 4
ROWS = 272
LOW = -2e30
ITEMS = REACH + 1
LAG = 2
BACK = (0, 2, 4, 1, 3)
MEET_LO = 3
WAIT_LO, WAIT_HI = 5, 4
X_LAG = 3


def kernel(
    q_ref, k_ref, v_ref, seg_ref, o_ref,
    q, segs, kv, edge, qseg, top, total, summed, in_sem,
    xz_send, xz_recv, y_send, y_recv, x_send, x_recv, c_send, c_recv, e_send, e_recv,
):
    me = lax.axis_index("ctx")
    off = lax.rem(me, BLOCKS)
    ring = me // BLOCKS
    c = lax.rem(me, 2)
    y = off // 2
    unit_scale = HEAD**-0.5 * math.log2(math.e)

    def at(dy):
        return 2 * lax.rem(y + dy + RING, RING) + c

    up = ring * BLOCKS + at(1)
    down = ring * BLOCKS + at(-1)
    twin = me + 1 - 2 * c

    def remote(src, dst, send, recv, to):
        return pltpu.make_async_remote_copy(
            src_ref=src, dst_ref=dst, send_sem=send, recv_sem=recv,
            device_id={"ctx": to}, device_id_type=MESH,
        )

    half = lax.rem(ring, 2)

    loads = [
        pltpu.make_async_copy(seg_ref, segs, in_sem.at[0]),
        pltpu.make_async_copy(k_ref, kv.at[0, off, pl.ds(0, TOK)], in_sem.at[1]),
        pltpu.make_async_copy(v_ref, kv.at[0, off, pl.ds(TOK, TOK)], in_sem.at[2]),
    ] + [
        pltpu.make_async_copy(
            q_ref.at[:, pl.ds(h * HEAD, HEAD)], q.at[pl.ds(h * TOK, TOK)], in_sem.at[3 + h]
        )
        for h in range(HEADS)
    ]
    for load in loads:
        load.start()

    has_edge = (off == 0) & (ring >= ITEMS)
    gives_edge = (off == BLOCKS - 1) & (ring + ITEMS < RINGS)

    barrier = pltpu.get_barrier_semaphore()

    def greet(to):
        pl.semaphore_signal(barrier, inc=1, device_id={"ctx": to}, device_id_type=MESH)

    def greet_half():
        @pl.when(ring >= 1)
        def _():
            greet(me - BLOCKS)

        @pl.when(ring + 1 < RINGS)
        def _():
            greet(me + BLOCKS)

        @pl.when(has_edge)
        def _():
            greet(me - REACH * BLOCKS - 1)

        @pl.when(gives_edge)
        def _():
            greet(me + REACH * BLOCKS + 1)

    def one(x):
        return x.astype(jnp.int32)

    others = one(ring >= 1) + one(ring + 1 < RINGS) + one(has_edge) + one(gives_edge)

    for to in (up, down, twin):
        greet(to)
    for d in (2, 4):

        @pl.when(ring >= d)
        def _():
            greet(me - d * BLOCKS)

    top[...] = jnp.full(top.shape, -1e30, jnp.float32)
    total[...] = jnp.zeros_like(total)
    summed[...] = jnp.zeros_like(summed)
    loads[0].wait()
    seg_row = segs[...].astype(jnp.float32)
    kv[0, off, pl.ds(2 * TOK, 16), :] = jnp.broadcast_to(seg_row, (16, TOK)).astype(jnp.bfloat16)
    qseg[...] = jnp.broadcast_to(seg_row, (TOK, TOK)).T
    for load in loads[1:]:
        load.wait()

    pl.semaphore_wait(
        barrier, 3 + one(ring + 2 < RINGS) + one(ring + 4 < RINGS) + half * others
    )
    greet_half()

    def delta(k):
        return lax.rem(2 * k, ITEMS)

    def xz(k, to):
        return remote(kv.at[0, off], kv.at[k, off], xz_send.at[k], xz_recv.at[k], to)

    def hop(k, dy, slot, to):
        b = at(dy)
        return remote(kv.at[k, b], kv.at[k, b], y_send.at[k, slot], y_recv.at[k, slot], to)

    def along(k, dy, slot):
        b = at(dy)
        return remote(
            kv.at[k, b], kv.at[k + 1, b], x_send.at[k, slot], x_recv.at[k + 1, slot],
            me + 2 * BLOCKS,
        )

    def cross(k, dy, slot):
        b = at(dy)
        return remote(kv.at[k, b], kv.at[k, b], c_send.at[k, slot], c_recv.at[k, slot], twin)

    def cross_in(k, dy, slot):
        b = 2 * lax.rem(y + dy + RING, RING) + 1 - c
        return remote(kv.at[k, b], kv.at[k, b], c_send.at[k, slot], c_recv.at[k, slot], twin)

    def from_x(k):
        return (k == 1) | (k == 4)

    def feeds_x(k):
        return ((k == 0) | (k == 3)) & (ring + 2 < RINGS)

    def pass_on(k, dy, slot):
        @pl.when(feeds_x(k))
        def _():
            along(k, dy, slot).start()

        cross(k, dy, slot).start()

    def x_in(k, slot):
        return remote(
            kv.at[k - 1, off], kv.at[k, off], x_send.at[k - 1, slot], x_recv.at[k, slot],
            me + 2 * BLOCKS,
        )

    def launch(k):
        hop(k, 0, 1, up).start()
        hop(k, 0, 4, down).start()
        pass_on(k, 0, 0)

    def edge_copy(to):
        return remote(kv.at[0, off], edge, e_send, e_recv, to)

    def send_half():
        @pl.when(ring + 1 < RINGS)
        def _():
            xz(3, me + BLOCKS).start()

        @pl.when(gives_edge)
        def _():
            edge_copy(me + REACH * BLOCKS + 1).start()

    launch(0)

    @pl.when(ring + 4 < RINGS)
    def _():
        xz(2, me + 4 * BLOCKS).start()

    @pl.when(half == 1)
    def _():
        send_half()

    def arrive(k, h):
        @pl.when(from_x(k))
        def _():
            if h == 4:
                x_in(k, 7).wait_recv()
                cross(k, 4, 7).start()
            else:
                x_in(k, h).wait_recv()
                cross(k, -h, h).start()
                x_in(k, 3 + h).wait_recv()
                cross(k, h, 3 + h).start()

        @pl.when(jnp.logical_not(from_x(k)))
        def _():
            if h == 4:
                hop(k, 4, 7, up).wait_recv()
                pass_on(k, 4, 7)
                return
            for side, to, core in ((-1, up, 0), (1, down, 1)):
                slot = h if side < 0 else 3 + h
                hop(k, side * h, slot, to).wait_recv()
                if h < 3:
                    hop(k, side * h, slot + 1, to).start()
                else:

                    @pl.when(c == core)
                    def _():
                        hop(k, side * 3, 7, to).start()

                pass_on(k, side * h, slot)

    lane = lax.broadcasted_iota(jnp.int32, (TOK, TOK), 1)
    row = lax.broadcasted_iota(jnp.int32, (TOK, TOK), 0)
    gap = row - lane

    def fold(blocks, ahead):
        keys = jnp.concatenate([b[pl.ds(0, TOK), :] for b in blocks], axis=0)
        values = jnp.concatenate([b[pl.ds(TOK, TOK), :] for b in blocks], axis=0)
        allowed = []
        for b, a in zip(blocks, ahead):
            seg = b[pl.ds(2 * TOK, 16), :].astype(jnp.float32)[0:1, :]
            allowed.append((seg == qseg[...]) & (gap >= a))
        score = lax.dot_general(
            q[...], keys, (((1,), (1,)), ((), ())), preferred_element_type=jnp.float32
        )
        rounded, keeps = [], []
        for h in range(HEADS):
            parts = [
                jnp.where(
                    allowed[n],
                    score[h * TOK : (h + 1) * TOK, n * TOK : (n + 1) * TOK] * unit_scale,
                    LOW,
                )
                for n in range(len(blocks))
            ]
            old = top[h]
            most = functools.reduce(jnp.maximum, parts)
            new = jnp.maximum(old, jnp.max(most, axis=1, keepdims=True))
            keep = jnp.exp2(old - new)
            weights = [jnp.exp2(p - new) for p in parts]
            top[h] = new
            total[h] = total[h] * keep + functools.reduce(jnp.add, weights)
            rounded.append(jnp.concatenate([w.astype(jnp.bfloat16) for w in weights], axis=1))
            keeps.append(keep)
        product = jnp.dot(
            jnp.concatenate(rounded, axis=0), values, preferred_element_type=jnp.float32
        )
        for h in range(HEADS):
            summed[h] = summed[h] * keeps[h] + product[h * TOK : (h + 1) * TOK]

    def unit(k, h):
        if h < 4:
            cross_in(k, -h, h).wait_recv()
            cross_in(k, h, 3 + h).wait_recv()
            first = (-h, h)
        else:
            cross_in(k, 0, 0).wait_recv()
            cross_in(k, 4, 7).wait_recv()
            first = (0, 4)
        blocks, ahead = [], []
        for dy in first:
            chip = lax.rem(y + dy + RING, RING)
            for core in range(2):
                b = 2 * chip + core
                blocks.append(kv.at[k, b])
                ahead.append((b - off - delta(k) * BLOCKS) * TOK)
        fold(blocks, ahead)

    def drain(k):
        @pl.when(jnp.logical_not(from_x(k)))
        def _():
            for slot in range(1, 8):
                hop(k, 0, slot, up).wait_send()

        @pl.when(feeds_x(k))
        def _():
            for slot in range(8):
                along(k, 0, slot).wait_send()

        for slot in range(8):
            cross(k, 0, slot).wait_send()

    wait = WAIT_LO + (WAIT_HI - WAIT_LO) * half
    last = wait + X_LAG

    def item(place):
        k = jnp.where(place == 0, 0, -1)
        k = jnp.where(place == 1, 2, k)
        k = jnp.where(place == X_LAG, 1, k)
        k = jnp.where(place == wait, 3, k)
        return jnp.where(place == last, 4, k)

    def here(k):
        return (k >= 0) & (ring >= delta(jnp.maximum(k, 0)))

    def begin(k):
        @pl.when(here(k) & from_x(k))
        def _():
            x_in(k, 0).wait_recv()
            cross(k, 0, 0).start()

        @pl.when(here(k) & jnp.logical_not(from_x(k)))
        def _():
            xz(k, me).wait_recv()
            launch(k)

    begin(jnp.int32(2))

    def step(j, _):
        @pl.when((half == 0) & (j == MEET_LO))
        def _():
            pl.semaphore_wait(barrier, others)
            send_half()

        for h in (4, 3, 2, 1):
            now = item(j - LAG * (h - 1))
            past = item(j - LAG * (h - 1) - 1)

            @pl.when(here(now))
            def _():
                arrive(now, h)

            @pl.when(here(past))
            def _():
                unit(past, h)

        begin(item(j + 2))
        done = item(j - LAG * 3 - 1)

        @pl.when(here(done))
        def _():
            drain(done)

        @pl.when(has_edge & (j == last + LAG))
        def _():
            edge_copy(me).wait_recv()
            fold([edge], [jnp.int32(-ITEMS * BLOCKS * TOK + (BLOCKS - 1) * TOK)])

        return 0

    lax.fori_loop(0, last + LAG * 3 + 2, step, 0)

    for h in range(HEADS):
        whole = jnp.sum(total[h], axis=1, keepdims=True)
        o_ref[:, h * HEAD : (h + 1) * HEAD] = (summed[h] * (1.0 / whole)).astype(jnp.bfloat16)

    for k in (2, 3):

        @pl.when(ring + BACK[k] < RINGS)
        def _():
            xz(k, me).wait_send()

    @pl.when(gives_edge)
    def _():
        edge_copy(me).wait_send()


def body(queries, keys, values, segment_ids):
    vmem = pl.BlockSpec(memory_space=pltpu.VMEM)
    return pl.pallas_call(
        kernel,
        out_shape=jax.ShapeDtypeStruct(queries.shape, queries.dtype),
        in_specs=[pl.BlockSpec(memory_space=pltpu.HBM)] * 4,
        out_specs=vmem,
        scratch_shapes=[
            pltpu.VMEM((HEADS * TOK, HEAD), jnp.bfloat16),
            pltpu.VMEM((1, TOK), jnp.int32),
            pltpu.VMEM((ITEMS, BLOCKS, ROWS, HEAD), jnp.bfloat16),
            pltpu.VMEM((ROWS, HEAD), jnp.bfloat16),
            pltpu.VMEM((TOK, TOK), jnp.float32),
            pltpu.VMEM((HEADS, TOK, HEAD), jnp.float32),
            pltpu.VMEM((HEADS, TOK, HEAD), jnp.float32),
            pltpu.VMEM((HEADS, TOK, HEAD), jnp.float32),
            pltpu.SemaphoreType.DMA((3 + HEADS,)),
            pltpu.SemaphoreType.DMA((ITEMS,)),
            pltpu.SemaphoreType.DMA((ITEMS,)),
            pltpu.SemaphoreType.DMA((ITEMS, 8)),
            pltpu.SemaphoreType.DMA((ITEMS, 8)),
            pltpu.SemaphoreType.DMA((ITEMS, 8)),
            pltpu.SemaphoreType.DMA((ITEMS, 8)),
            pltpu.SemaphoreType.DMA((ITEMS, 8)),
            pltpu.SemaphoreType.DMA((ITEMS, 8)),
            pltpu.SemaphoreType.DMA,
            pltpu.SemaphoreType.DMA,
        ],
        compiler_params=pltpu.CompilerParams(
            collective_id=0, has_side_effects=True, vmem_limit_bytes=60 << 20
        ),
        name="attend_ring",
    )(queries, keys, values, segment_ids.reshape(1, TOK))


def solution(mesh):
    return jax.shard_map(
        body,
        mesh=mesh,
        in_specs=(P("ctx", "kvh"), P("ctx", "kvh"), P("ctx", "kvh"), P("ctx")),
        out_specs=P("ctx", "kvh"),
        check_vma=False,
    )
```

```python
import functools
import math

import jax
import jax.numpy as jnp
from jax import lax
from jax.experimental import pallas as pl
from jax.experimental.pallas import tpu as pltpu
from jax.sharding import PartitionSpec as P

MESH = pl.DeviceIdType.MESH
RING = 8
BLOCKS = 2 * RING
RINGS = 8
REACH = 4
TOK = 128
HEAD = 128
HEADS = 4
ROWS = 272
LOW = -2e30
ITEMS = REACH + 1
BACK = (0, 2, 4, 1, 3)
PLACE = {0: 0, 4: 1, -1: 2, 1: 3, -2: 4, 2: 5, -3: 6, 3: 7}
MEET = 3
LOW_STEPS, HIGH_STEPS = (0, 3, 1, 5, 8), (0, 3, 1, 4, 7)
LAG = 2

def kernel(
    q_ref, k_ref, v_ref, seg_ref, o_ref,
    q, segs, kv, edge, qseg, top, total, summed, in_sem,
    xz_send, xz_recv, y_send, y_recv, x_send, x_recv, c_send, c_recv, e_send, e_recv,
):
    me = lax.axis_index("ctx")
    off = lax.rem(me, BLOCKS)
    ring = me // BLOCKS
    c = lax.rem(me, 2)
    y = off // 2
    unit_scale = HEAD**-0.5 * math.log2(math.e)

    def at(dy):
        return 2 * lax.rem(y + dy + RING, RING) + c

    up = ring * BLOCKS + at(1)
    down = ring * BLOCKS + at(-1)
    twin = me + 1 - 2 * c

    def remote(src, dst, send, recv, to):
        return pltpu.make_async_remote_copy(
            src_ref=src, dst_ref=dst, send_sem=send, recv_sem=recv,
            device_id={"ctx": to}, device_id_type=MESH,
        )

    half = lax.rem(ring, 2)

    loads = [
        pltpu.make_async_copy(seg_ref, segs, in_sem.at[0]),
        pltpu.make_async_copy(k_ref, kv.at[0, c, 0, pl.ds(0, TOK)], in_sem.at[1]),
        pltpu.make_async_copy(v_ref, kv.at[0, c, 0, pl.ds(TOK, TOK)], in_sem.at[2]),
    ] + [
        pltpu.make_async_copy(
            q_ref.at[:, pl.ds(h * HEAD, HEAD)], q.at[pl.ds(h * TOK, TOK)], in_sem.at[3 + h]
        )
        for h in range(HEADS)
    ]
    for load in loads:
        load.start()

    has_edge = (off == 0) & (ring >= ITEMS)
    gives_edge = (off == BLOCKS - 1) & (ring + ITEMS < RINGS)

    barrier = pltpu.get_barrier_semaphore()

    def greet(to):
        pl.semaphore_signal(barrier, inc=1, device_id={"ctx": to}, device_id_type=MESH)

    def greet_half():
        @pl.when(ring >= 1)
        def _():
            greet(me - BLOCKS)

        @pl.when(ring + 1 < RINGS)
        def _():
            greet(me + BLOCKS)

        @pl.when(has_edge)
        def _():
            greet(me - REACH * BLOCKS - 1)

        @pl.when(gives_edge)
        def _():
            greet(me + REACH * BLOCKS + 1)

    def one(x):
        return x.astype(jnp.int32)

    others = one(ring >= 1) + one(ring + 1 < RINGS) + one(has_edge) + one(gives_edge)

    for to in (up, down, twin):
        greet(to)
    for d in (2, 4):

        @pl.when(ring >= d)
        def _():
            greet(me - d * BLOCKS)

    top[...] = jnp.full(top.shape, -1e30, jnp.float32)
    total[...] = jnp.zeros_like(total)
    summed[...] = jnp.zeros_like(summed)
    loads[0].wait()
    seg_row = segs[...].astype(jnp.float32)
    kv[0, c, 0, pl.ds(2 * TOK, 16), :] = jnp.broadcast_to(seg_row, (16, TOK)).astype(jnp.bfloat16)
    qseg[...] = jnp.broadcast_to(seg_row, (TOK, TOK)).T
    for load in loads[1:]:
        load.wait()

    pl.semaphore_wait(
        barrier, 3 + one(ring + 2 < RINGS) + one(ring + 4 < RINGS) + half * others
    )
    greet_half()

    def delta(k):
        return lax.rem(2 * k, ITEMS)

    def xz(k, to):
        return remote(kv.at[0, c, 0], kv.at[k, c, 0], xz_send.at[k], xz_recv.at[k], to)

    def hop(k, here, there, to):
        return remote(
            kv.at[k, c, PLACE[here]], kv.at[k, c, PLACE[there]],
            y_send.at[k], y_recv.at[k, PLACE[there]], to,
        )

    def pair(h):
        return pl.ds(2 * (h % 4), 2)

    def along(k, h):
        return remote(
            kv.at[k, c, pair(h)], kv.at[k + 1, c, pair(h)],
            x_send.at[k], x_recv.at[k + 1, h % 4], me + 2 * BLOCKS,
        )

    def cross(k, h, core):
        blocks = kv.at[k, core, pair(h)]
        return remote(blocks, blocks, c_send.at[k], c_recv.at[k, h % 4], twin)

    def from_x(k):
        return (k == 1) | ((k == 4) & (c == 0))

    def feeds_x(k):
        return ((k == 0) | ((k == 3) & (c == 0))) & (ring + 2 < RINGS)

    def launch(k):
        hop(k, 0, -1, up).start()
        hop(k, 0, 1, down).start()

    def edge_copy(to):
        return remote(kv.at[0, c, 0], edge, e_send, e_recv, to)

    def send_half():
        @pl.when(ring + 1 < RINGS)
        def _():
            xz(3, me + BLOCKS).start()

        @pl.when(gives_edge)
        def _():
            edge_copy(me + REACH * BLOCKS + 1).start()

    @pl.when(half == 1)
    def _():
        send_half()

    launch(0)

    @pl.when(ring + 4 < RINGS)
    def _():
        xz(2, me + 4 * BLOCKS).start()

    def arrive(k, h):
        @pl.when(from_x(k))
        def _():
            along(k - 1, h).wait_recv()

        @pl.when(jnp.logical_not(from_x(k)))
        def _():
            if h == 4:
                hop(k, 0, 4, up).wait_recv()
            else:
                for side, to, core in ((-1, up, 0), (1, down, 1)):
                    hop(k, 0, side * h, to).wait_recv()
                    if h < 3:
                        hop(k, side * h, side * (h + 1), to).start()
                    else:

                        @pl.when(c == core)
                        def _():
                            hop(k, side * 3, 4, to).start()

        cross(k, h, c).start()

        @pl.when(feeds_x(k))
        def _():
            along(k, h).start()

    lane = lax.broadcasted_iota(jnp.int32, (TOK, TOK), 1)
    row = lax.broadcasted_iota(jnp.int32, (TOK, TOK), 0)
    gap = row - lane

    def fold(blocks, ahead):
        keys = jnp.concatenate([b[pl.ds(0, TOK), :] for b in blocks], axis=0)
        values = jnp.concatenate([b[pl.ds(TOK, TOK), :] for b in blocks], axis=0)
        allowed = []
        for b, a in zip(blocks, ahead):
            seg = b[pl.ds(2 * TOK, 16), :].astype(jnp.float32)[0:1, :]
            allowed.append((seg == qseg[...]) & (gap >= a))
        score = lax.dot_general(
            q[...], keys, (((1,), (1,)), ((), ())), preferred_element_type=jnp.float32
        )
        rounded, keeps = [], []
        for h in range(HEADS):
            parts = [
                jnp.where(
                    allowed[n],
                    score[h * TOK : (h + 1) * TOK, n * TOK : (n + 1) * TOK] * unit_scale,
                    LOW,
                )
                for n in range(len(blocks))
            ]
            old = top[h]
            most = functools.reduce(jnp.maximum, parts)
            new = jnp.maximum(old, jnp.max(most, axis=1, keepdims=True))
            keep = jnp.exp2(old - new)
            weights = [jnp.exp2(p - new) for p in parts]
            top[h] = new
            total[h] = total[h] * keep + functools.reduce(jnp.add, weights)
            rounded.append(jnp.concatenate([w.astype(jnp.bfloat16) for w in weights], axis=1))
            keeps.append(keep)
        product = jnp.dot(
            jnp.concatenate(rounded, axis=0), values, preferred_element_type=jnp.float32
        )
        for h in range(HEADS):
            summed[h] = summed[h] * keeps[h] + product[h * TOK : (h + 1) * TOK]

    def unit(k, h):
        cross(k, h, 1 - c).wait_recv()
        blocks, ahead = [], []
        for dy in (0, 4) if h == 4 else (-h, h):
            for core in range(2):
                b = 2 * lax.rem(y + dy + RING, RING) + core
                blocks.append(kv.at[k, core, PLACE[dy]])
                ahead.append((b - off - delta(k) * BLOCKS) * TOK)
        fold(blocks, ahead)

    def drain(k):
        whole = kv.at[k, c]

        @pl.when(jnp.logical_not(from_x(k)))
        def _():
            sent = kv.at[k, c, pl.ds(0, 7)]
            remote(sent, sent, y_send.at[k], y_recv.at[k, 0], up).wait_send()

        @pl.when(feeds_x(k))
        def _():
            remote(whole, whole, x_send.at[k], x_recv.at[k, 0], twin).wait_send()

        remote(whole, whole, c_send.at[k], c_recv.at[k, 0], twin).wait_send()

    def pick(j):
        k = jnp.int32(-1)
        for n, (a, b) in enumerate(zip(LOW_STEPS, HIGH_STEPS)):
            k = jnp.where(j == a + (b - a) * half, n, k)
        return k

    def here(k):
        return (k >= 0) & (ring >= delta(jnp.maximum(k, 0)))

    def xy():
        return remote(
            kv.at[3, c, 0], kv.at[4, c, 0], xz_send.at[4], xz_recv.at[4], me + 2 * BLOCKS
        )

    hands_on = (c == 1) & (ring >= 1) & (ring + 2 < RINGS)

    def begin(k):
        @pl.when(here(k) & jnp.logical_not(from_x(k)))
        def _():
            xz(k, me).wait_recv()

            @pl.when((k == 3) & hands_on)
            def _():
                xy().start()

            launch(k)

    begin(jnp.int32(2))

    def step(j, _):
        @pl.when((half == 0) & (j == MEET))
        def _():
            pl.semaphore_wait(barrier, others)
            send_half()

        for h in (4, 3, 2, 1):
            now = pick(j - LAG * (h - 1))
            past = pick(j - LAG * (h - 1) - 1)

            @pl.when(here(now))
            def _():
                arrive(now, h)

            @pl.when(here(past))
            def _():
                unit(past, h)

        begin(pick(j + 2))
        done = pick(j - LAG * 3 - 1)

        @pl.when(here(done))
        def _():
            drain(done)

        @pl.when(has_edge & (j == LOW_STEPS[4] + LAG))
        def _():
            edge_copy(me).wait_recv()
            fold([edge], [jnp.int32(-ITEMS * BLOCKS * TOK + (BLOCKS - 1) * TOK)])

        return 0

    lax.fori_loop(0, max(LOW_STEPS[4], HIGH_STEPS[4]) + LAG * 3 + 2, step, 0)

    for h in range(HEADS):
        whole = jnp.sum(total[h], axis=1, keepdims=True)
        o_ref[:, h * HEAD : (h + 1) * HEAD] = (summed[h] * (1.0 / whole)).astype(jnp.bfloat16)

    for k in (2, 3):

        @pl.when(ring + BACK[k] < RINGS)
        def _():
            xz(k, me).wait_send()

    @pl.when(hands_on)
    def _():
        xy().wait_send()

    @pl.when(gives_edge)
    def _():
        edge_copy(me).wait_send()


def body(queries, keys, values, segment_ids):
    vmem = pl.BlockSpec(memory_space=pltpu.VMEM)
    return pl.pallas_call(
        kernel,
        out_shape=jax.ShapeDtypeStruct(queries.shape, queries.dtype),
        in_specs=[pl.BlockSpec(memory_space=pltpu.HBM)] * 4,
        out_specs=vmem,
        scratch_shapes=[
            pltpu.VMEM((HEADS * TOK, HEAD), jnp.bfloat16),
            pltpu.VMEM((1, TOK), jnp.int32),
            pltpu.VMEM((ITEMS, 2, RING, ROWS, HEAD), jnp.bfloat16),
            pltpu.VMEM((ROWS, HEAD), jnp.bfloat16),
            pltpu.VMEM((TOK, TOK), jnp.float32),
            pltpu.VMEM((HEADS, TOK, HEAD), jnp.float32),
            pltpu.VMEM((HEADS, TOK, HEAD), jnp.float32),
            pltpu.VMEM((HEADS, TOK, HEAD), jnp.float32),
            pltpu.SemaphoreType.DMA((3 + HEADS,)),
            pltpu.SemaphoreType.DMA((ITEMS,)),
            pltpu.SemaphoreType.DMA((ITEMS,)),
            pltpu.SemaphoreType.DMA((ITEMS,)),
            pltpu.SemaphoreType.DMA((ITEMS, RING)),
            pltpu.SemaphoreType.DMA((ITEMS,)),
            pltpu.SemaphoreType.DMA((ITEMS, 4)),
            pltpu.SemaphoreType.DMA((ITEMS,)),
            pltpu.SemaphoreType.DMA((ITEMS, 4)),
            pltpu.SemaphoreType.DMA,
            pltpu.SemaphoreType.DMA,
        ],
        compiler_params=pltpu.CompilerParams(
            collective_id=0, has_side_effects=True, vmem_limit_bytes=60 << 20
        ),
        name="attend_ring",
    )(queries, keys, values, segment_ids.reshape(1, TOK))


def solution(mesh):
    return jax.shard_map(
        body,
        mesh=mesh,
        in_specs=(P("ctx", "kvh"), P("ctx", "kvh"), P("ctx", "kvh"), P("ctx")),
        out_specs=P("ctx", "kvh"),
        check_vma=False,
    )
```

```python
import functools
import math

import jax
import jax.numpy as jnp
from jax import lax
from jax.experimental import pallas as pl
from jax.experimental.pallas import tpu as pltpu
from jax.sharding import PartitionSpec as P

MESH = pl.DeviceIdType.MESH
RING = 8
BLOCKS = 2 * RING
RINGS = 8
REACH = 4
TOK = 128
HEAD = 128
HEADS = 4
ROWS = 272
LOW = -2e30
ITEMS = REACH + 1
BACK = (0, 2, 4, 1, 3)
PLACE = {0: 0, 4: 1, -1: 2, 1: 3, -2: 4, 2: 5, -3: 6, 3: 7}
MEET = 2
LOW_STEPS, HIGH_STEPS = (0, 3, 1, 5, 8), (0, 3, 1, 4, 7)
LAG = 2

def kernel(
    q_ref, k_ref, v_ref, seg_ref, o_ref,
    q, segs, kv, edge, qseg, top, total, summed, in_sem,
    xz_send, xz_recv, y_send, y_recv, x_send, x_recv, c_send, c_recv, t_send, e_send, e_recv,
):
    me = lax.axis_index("ctx")
    off = lax.rem(me, BLOCKS)
    ring = me // BLOCKS
    c = lax.rem(me, 2)
    y = off // 2
    unit_scale = HEAD**-0.5 * math.log2(math.e)

    def at(dy):
        return 2 * lax.rem(y + dy + RING, RING) + c

    up = ring * BLOCKS + at(1)
    down = ring * BLOCKS + at(-1)
    twin = me + 1 - 2 * c

    def remote(src, dst, send, recv, to):
        return pltpu.make_async_remote_copy(
            src_ref=src, dst_ref=dst, send_sem=send, recv_sem=recv,
            device_id={"ctx": to}, device_id_type=MESH,
        )

    half = lax.rem(ring, 2)

    loads = [
        pltpu.make_async_copy(seg_ref, segs, in_sem.at[0]),
        pltpu.make_async_copy(k_ref, kv.at[0, c, 0, pl.ds(0, TOK)], in_sem.at[1]),
        pltpu.make_async_copy(v_ref, kv.at[0, c, 0, pl.ds(TOK, TOK)], in_sem.at[2]),
    ] + [
        pltpu.make_async_copy(
            q_ref.at[:, pl.ds(h * HEAD, HEAD)], q.at[pl.ds(h * TOK, TOK)], in_sem.at[3 + h]
        )
        for h in range(HEADS)
    ]
    for load in loads:
        load.start()

    kv[2] = jnp.zeros(kv.shape[1:], kv.dtype)

    has_edge = (off == 0) & (ring >= ITEMS)
    gives_edge = (off == BLOCKS - 1) & (ring + ITEMS < RINGS)

    barrier = pltpu.get_barrier_semaphore()

    def greet(to):
        pl.semaphore_signal(barrier, inc=1, device_id={"ctx": to}, device_id_type=MESH)

    def greet_half():
        @pl.when(ring >= 1)
        def _():
            greet(me - BLOCKS)

        @pl.when(ring + 1 < RINGS)
        def _():
            greet(me + BLOCKS)

        @pl.when(has_edge)
        def _():
            greet(me - REACH * BLOCKS - 1)

        @pl.when(gives_edge)
        def _():
            greet(me + REACH * BLOCKS + 1)

    def one(x):
        return x.astype(jnp.int32)

    others = one(ring >= 1) + one(ring + 1 < RINGS) + one(has_edge) + one(gives_edge)

    for to in (up, down, twin):
        greet(to)
    for d in (2, 4):

        @pl.when(ring >= d)
        def _():
            greet(me - d * BLOCKS)

    top[...] = jnp.full(top.shape, -1e30, jnp.float32)
    total[...] = jnp.zeros_like(total)
    summed[...] = jnp.zeros_like(summed)
    loads[0].wait()
    seg_row = segs[...].astype(jnp.float32)
    kv[0, c, 0, pl.ds(2 * TOK, 16), :] = jnp.broadcast_to(seg_row, (16, TOK)).astype(jnp.bfloat16)
    qseg[...] = jnp.broadcast_to(seg_row, (TOK, TOK)).T
    for load in loads[1:]:
        load.wait()

    pl.semaphore_wait(
        barrier, 3 + one(ring + 2 < RINGS) + one(ring + 4 < RINGS) + half * others
    )
    greet_half()

    def delta(k):
        return lax.rem(2 * k, ITEMS)

    def xz(k, to):
        return remote(kv.at[0, c, 0], kv.at[k, c, 0], xz_send.at[k], xz_recv.at[k], to)

    def hop(k, here, there, to):
        return remote(
            kv.at[k, c, PLACE[here]], kv.at[k, c, PLACE[there]],
            y_send.at[k], y_recv.at[k, PLACE[there]], to,
        )

    def trim(here, there, to, n):
        return remote(
            kv.at[2, c, PLACE[here]], kv.at[2, c, PLACE[there]],
            t_send.at[n], y_recv.at[2, PLACE[there]], to,
        )

    def source(h):
        return lax.rem(y - h + RING, RING)

    def trims():
        out = []
        for h in range(3):
            go = source(h) >= 5
            if h == 0:
                go = go | (c == 1)
            out.append((go, functools.partial(trim, -h, -h - 1, up, h)))
        for h in range(4):
            out.append(((y + h < RING) & (y >= 1), functools.partial(trim, h, h + 1, down, 3 + h)))
        return out

    def start_trim(n):
        go, copy = trims()[n]

        @pl.when(go)
        def _():
            copy().start()

    def arrive_trim(h):
        if h == 4:

            @pl.when(y < 4)
            def _():
                hop(2, 0, 4, down).wait_recv()

            return
        comes = source(h) >= 5
        if h == 1:
            comes = comes | (c == 1)

        @pl.when(comes)
        def _():
            hop(2, 0, -h, up).wait_recv()

        if h < 3:
            start_trim(h)

        @pl.when(y + h < RING)
        def _():
            hop(2, 0, h, down).wait_recv()

        start_trim(3 + h)

    def absent(dy, core):
        if dy == 0:
            return jnp.bool_(False)
        if dy > 0:
            return y + dy >= RING
        if dy == -1 and core == 1:
            return jnp.bool_(False)
        return y + dy >= 0

    def pair(h):
        return pl.ds(2 * (h % 4), 2)

    def along(k, h):
        return remote(
            kv.at[k, c, pair(h)], kv.at[k + 1, c, pair(h)],
            x_send.at[k], x_recv.at[k + 1, h % 4], me + 2 * BLOCKS,
        )

    def cross(k, h, core):
        blocks = kv.at[k, core, pair(h)]
        return remote(blocks, blocks, c_send.at[k], c_recv.at[k, h % 4], twin)

    def from_x(k):
        return (k == 1) | ((k == 4) & (c == 0))

    def feeds_x(k):
        return ((k == 0) | ((k == 3) & (c == 0))) & (ring + 2 < RINGS)

    def launch(k):
        @pl.when(k == 2)
        def _():
            start_trim(0)
            start_trim(3)

        @pl.when(k != 2)
        def _():
            hop(k, 0, -1, up).start()
            hop(k, 0, 1, down).start()

    def edge_copy(to):
        return remote(kv.at[0, c, 0], edge, e_send, e_recv, to)

    def send_half():
        @pl.when(ring + 1 < RINGS)
        def _():
            xz(3, me + BLOCKS).start()

        @pl.when(gives_edge)
        def _():
            edge_copy(me + REACH * BLOCKS + 1).start()

    @pl.when(half == 1)
    def _():
        send_half()

    launch(0)

    @pl.when(ring + 4 < RINGS)
    def _():
        xz(2, me + 4 * BLOCKS).start()

    def arrive(k, h):
        @pl.when(from_x(k))
        def _():
            along(k - 1, h).wait_recv()

        @pl.when(k == 2)
        def _():
            arrive_trim(h)

        @pl.when(jnp.logical_not(from_x(k)) & (k != 2))
        def _():
            if h == 4:
                hop(k, 0, 4, up).wait_recv()
            else:
                for side, to, core in ((-1, up, 0), (1, down, 1)):
                    hop(k, 0, side * h, to).wait_recv()
                    if h < 3:
                        hop(k, side * h, side * (h + 1), to).start()
                    else:

                        @pl.when(c == core)
                        def _():
                            hop(k, side * 3, 4, to).start()

        cross(k, h, c).start()

        @pl.when(feeds_x(k))
        def _():
            along(k, h).start()

    lane = lax.broadcasted_iota(jnp.int32, (TOK, TOK), 1)
    row = lax.broadcasted_iota(jnp.int32, (TOK, TOK), 0)
    gap = row - lane

    def fold(blocks, ahead):
        keys = jnp.concatenate([b[pl.ds(0, TOK), :] for b in blocks], axis=0)
        values = jnp.concatenate([b[pl.ds(TOK, TOK), :] for b in blocks], axis=0)
        allowed = []
        for b, a in zip(blocks, ahead):
            seg = b[pl.ds(2 * TOK, 16), :].astype(jnp.float32)[0:1, :]
            allowed.append((seg == qseg[...]) & (gap >= a))
        score = lax.dot_general(
            q[...], keys, (((1,), (1,)), ((), ())), preferred_element_type=jnp.float32
        )
        rounded, keeps = [], []
        for h in range(HEADS):
            parts = [
                jnp.where(
                    allowed[n],
                    score[h * TOK : (h + 1) * TOK, n * TOK : (n + 1) * TOK] * unit_scale,
                    LOW,
                )
                for n in range(len(blocks))
            ]
            old = top[h]
            most = functools.reduce(jnp.maximum, parts)
            new = jnp.maximum(old, jnp.max(most, axis=1, keepdims=True))
            keep = jnp.exp2(old - new)
            weights = [jnp.exp2(p - new) for p in parts]
            top[h] = new
            total[h] = total[h] * keep + functools.reduce(jnp.add, weights)
            rounded.append(jnp.concatenate([w.astype(jnp.bfloat16) for w in weights], axis=1))
            keeps.append(keep)
        product = jnp.dot(
            jnp.concatenate(rounded, axis=0), values, preferred_element_type=jnp.float32
        )
        for h in range(HEADS):
            summed[h] = summed[h] * keeps[h] + product[h * TOK : (h + 1) * TOK]

    def unit(k, h):
        cross(k, h, 1 - c).wait_recv()
        blocks, ahead = [], []
        for dy in (0, 4) if h == 4 else (-h, h):
            for core in range(2):
                b = 2 * lax.rem(y + dy + RING, RING) + core
                blocks.append(kv.at[k, core, PLACE[dy]])
                a = (b - off - delta(k) * BLOCKS) * TOK
                ahead.append(jnp.where((k == 2) & absent(dy, core), TOK, a))
        fold(blocks, ahead)

    def drain(k):
        whole = kv.at[k, c]

        @pl.when(k == 2)
        def _():
            for go, copy in trims():

                @pl.when(go)
                def _():
                    copy().wait_send()

        @pl.when(jnp.logical_not(from_x(k)) & (k != 2))
        def _():
            sent = kv.at[k, c, pl.ds(0, 7)]
            remote(sent, sent, y_send.at[k], y_recv.at[k, 0], up).wait_send()

        @pl.when(feeds_x(k))
        def _():
            remote(whole, whole, x_send.at[k], x_recv.at[k, 0], twin).wait_send()

        remote(whole, whole, c_send.at[k], c_recv.at[k, 0], twin).wait_send()

    def pick(j):
        k = jnp.int32(-1)
        for n, (a, b) in enumerate(zip(LOW_STEPS, HIGH_STEPS)):
            k = jnp.where(j == a + (b - a) * half, n, k)
        return k

    def here(k):
        return (k >= 0) & (ring >= delta(jnp.maximum(k, 0)))

    def xy():
        return remote(
            kv.at[3, c, 0], kv.at[4, c, 0], xz_send.at[4], xz_recv.at[4], me + 2 * BLOCKS
        )

    hands_on = (c == 1) & (ring >= 1) & (ring + 2 < RINGS)

    def begin(k):
        @pl.when(here(k) & jnp.logical_not(from_x(k)))
        def _():
            xz(k, me).wait_recv()

            @pl.when((k == 3) & hands_on)
            def _():
                xy().start()

            launch(k)

    begin(jnp.int32(2))

    def step(j, _):
        @pl.when((half == 0) & (j == MEET))
        def _():
            pl.semaphore_wait(barrier, others)
            send_half()

        for h in (4, 3, 2, 1):
            now = pick(j - LAG * (h - 1))
            past = pick(j - LAG * (h - 1) - 2)

            @pl.when(here(now))
            def _():
                arrive(now, h)

            @pl.when(here(past))
            def _():
                unit(past, h)

        begin(pick(j + 2))
        done = pick(j - LAG * 3 - 1)

        @pl.when(here(done))
        def _():
            drain(done)

        @pl.when(has_edge & (j == LOW_STEPS[4] + LAG))
        def _():
            edge_copy(me).wait_recv()
            fold([edge], [jnp.int32(-ITEMS * BLOCKS * TOK + (BLOCKS - 1) * TOK)])

        return 0

    lax.fori_loop(0, max(LOW_STEPS[4], HIGH_STEPS[4]) + LAG * 3 + 3, step, 0)

    for h in range(HEADS):
        whole = jnp.sum(total[h], axis=1, keepdims=True)
        o_ref[:, h * HEAD : (h + 1) * HEAD] = (summed[h] * (1.0 / whole)).astype(jnp.bfloat16)

    for k in (2, 3):

        @pl.when(ring + BACK[k] < RINGS)
        def _():
            xz(k, me).wait_send()

    @pl.when(hands_on)
    def _():
        xy().wait_send()

    @pl.when(gives_edge)
    def _():
        edge_copy(me).wait_send()


def body(queries, keys, values, segment_ids):
    vmem = pl.BlockSpec(memory_space=pltpu.VMEM)
    return pl.pallas_call(
        kernel,
        out_shape=jax.ShapeDtypeStruct(queries.shape, queries.dtype),
        in_specs=[pl.BlockSpec(memory_space=pltpu.HBM)] * 4,
        out_specs=vmem,
        scratch_shapes=[
            pltpu.VMEM((HEADS * TOK, HEAD), jnp.bfloat16),
            pltpu.VMEM((1, TOK), jnp.int32),
            pltpu.VMEM((ITEMS, 2, RING, ROWS, HEAD), jnp.bfloat16),
            pltpu.VMEM((ROWS, HEAD), jnp.bfloat16),
            pltpu.VMEM((TOK, TOK), jnp.float32),
            pltpu.VMEM((HEADS, TOK, HEAD), jnp.float32),
            pltpu.VMEM((HEADS, TOK, HEAD), jnp.float32),
            pltpu.VMEM((HEADS, TOK, HEAD), jnp.float32),
            pltpu.SemaphoreType.DMA((3 + HEADS,)),
            pltpu.SemaphoreType.DMA((ITEMS,)),
            pltpu.SemaphoreType.DMA((ITEMS,)),
            pltpu.SemaphoreType.DMA((ITEMS,)),
            pltpu.SemaphoreType.DMA((ITEMS, RING)),
            pltpu.SemaphoreType.DMA((ITEMS,)),
            pltpu.SemaphoreType.DMA((ITEMS, 4)),
            pltpu.SemaphoreType.DMA((ITEMS,)),
            pltpu.SemaphoreType.DMA((ITEMS, 4)),
            pltpu.SemaphoreType.DMA((7,)),
            pltpu.SemaphoreType.DMA,
            pltpu.SemaphoreType.DMA,
        ],
        compiler_params=pltpu.CompilerParams(
            collective_id=0, has_side_effects=True, vmem_limit_bytes=60 << 20
        ),
        name="attend_ring",
    )(queries, keys, values, segment_ids.reshape(1, TOK))


def solution(mesh):
    return jax.shard_map(
        body,
        mesh=mesh,
        in_specs=(P("ctx", "kvh"), P("ctx", "kvh"), P("ctx", "kvh"), P("ctx")),
        out_specs=P("ctx", "kvh"),
        check_vma=False,
    )
```

```python
import functools
import math

import jax
import jax.numpy as jnp
from jax import lax
from jax.experimental import pallas as pl
from jax.experimental.pallas import tpu as pltpu
from jax.sharding import PartitionSpec as P

MESH = pl.DeviceIdType.MESH
RING = 8
BLOCKS = 2 * RING
RINGS = 8
REACH = 4
TOK = 128
HEAD = 128
HEADS = 4
ROWS = 272
LOW = -2e30
ITEMS = REACH + 1
BACK = (0, 2, 4, 1, 3)
PLACE = {0: 0, 4: 1, -1: 2, 1: 3, -2: 4, 2: 5, -3: 6, 3: 7}
MEET = 2
LOW_STEPS, HIGH_STEPS = (0, 3, 1, 4, 7), (0, 3, 1, 4, 7)
LAG = 2

def kernel(
    q_ref, k_ref, v_ref, seg_ref, o_ref,
    q, segs, kv, edge, qseg, top, total, summed, in_sem,
    xz_send, xz_recv, y_send, y_recv, x_send, x_recv, c_send, c_recv, t_send, e_send, e_recv,
):
    me = lax.axis_index("ctx")
    off = lax.rem(me, BLOCKS)
    ring = me // BLOCKS
    c = lax.rem(me, 2)
    y = off // 2
    unit_scale = HEAD**-0.5 * math.log2(math.e)

    def at(dy):
        return 2 * lax.rem(y + dy + RING, RING) + c

    up = ring * BLOCKS + at(1)
    down = ring * BLOCKS + at(-1)
    twin = me + 1 - 2 * c

    def remote(src, dst, send, recv, to):
        return pltpu.make_async_remote_copy(
            src_ref=src, dst_ref=dst, send_sem=send, recv_sem=recv,
            device_id={"ctx": to}, device_id_type=MESH,
        )

    half = lax.rem(ring, 2)

    loads = [
        pltpu.make_async_copy(seg_ref, segs, in_sem.at[0]),
        pltpu.make_async_copy(k_ref, kv.at[0, c, 0, pl.ds(0, TOK)], in_sem.at[1]),
        pltpu.make_async_copy(v_ref, kv.at[0, c, 0, pl.ds(TOK, TOK)], in_sem.at[2]),
    ] + [
        pltpu.make_async_copy(
            q_ref.at[:, pl.ds(h * HEAD, HEAD)], q.at[pl.ds(h * TOK, TOK)], in_sem.at[3 + h]
        )
        for h in range(HEADS)
    ]
    for load in loads:
        load.start()

    kv[2] = jnp.zeros(kv.shape[1:], kv.dtype)

    has_edge = (off == 0) & (ring >= ITEMS)
    gives_edge = (off == BLOCKS - 1) & (ring + ITEMS < RINGS)

    barrier = pltpu.get_barrier_semaphore()

    def greet(to):
        pl.semaphore_signal(barrier, inc=1, device_id={"ctx": to}, device_id_type=MESH)

    def greet_half():
        @pl.when(ring >= 1)
        def _():
            greet(me - BLOCKS)

        @pl.when(ring + 1 < RINGS)
        def _():
            greet(me + BLOCKS)

        @pl.when(has_edge)
        def _():
            greet(me - REACH * BLOCKS - 1)

        @pl.when(gives_edge)
        def _():
            greet(me + REACH * BLOCKS + 1)

    def one(x):
        return x.astype(jnp.int32)

    others = one(ring >= 1) + one(ring + 1 < RINGS) + one(has_edge) + one(gives_edge)

    for to in (up, down, twin):
        greet(to)
    for d in (2, 4):

        @pl.when(ring >= d)
        def _():
            greet(me - d * BLOCKS)

    top[...] = jnp.full(top.shape, -1e30, jnp.float32)
    total[...] = jnp.zeros_like(total)
    summed[...] = jnp.zeros_like(summed)
    loads[0].wait()
    seg_row = segs[...].astype(jnp.float32)
    kv[0, c, 0, pl.ds(2 * TOK, 16), :] = jnp.broadcast_to(seg_row, (16, TOK)).astype(jnp.bfloat16)
    qseg[...] = jnp.broadcast_to(seg_row, (TOK, TOK)).T
    for load in loads[1:]:
        load.wait()

    pl.semaphore_wait(
        barrier, 3 + one(ring + 2 < RINGS) + one(ring + 4 < RINGS) + half * others
    )
    greet_half()

    def delta(k):
        return lax.rem(2 * k, ITEMS)

    def xz(k, to):
        return remote(kv.at[0, c, 0], kv.at[k, c, 0], xz_send.at[k], xz_recv.at[k], to)

    def hop(k, here, there, to):
        return remote(
            kv.at[k, c, PLACE[here]], kv.at[k, c, PLACE[there]],
            y_send.at[k], y_recv.at[k, PLACE[there]], to,
        )

    def trim(here, there, to, n):
        return remote(
            kv.at[2, c, PLACE[here]], kv.at[2, c, PLACE[there]],
            t_send.at[n], y_recv.at[2, PLACE[there]], to,
        )

    def source(h):
        return lax.rem(y - h + RING, RING)

    def trims():
        out = []
        for h in range(3):
            go = source(h) >= 5
            if h == 0:
                go = go | (c == 1)
            out.append((go, functools.partial(trim, -h, -h - 1, up, h)))
        for h in range(4):
            out.append(((y + h < RING) & (y >= 1), functools.partial(trim, h, h + 1, down, 3 + h)))
        return out

    def start_trim(n):
        go, copy = trims()[n]

        @pl.when(go)
        def _():
            copy().start()

    def arrive_trim(h):
        if h == 4:

            @pl.when(y < 4)
            def _():
                hop(2, 0, 4, down).wait_recv()

            return
        comes = source(h) >= 5
        if h == 1:
            comes = comes | (c == 1)

        @pl.when(comes)
        def _():
            hop(2, 0, -h, up).wait_recv()

        if h < 3:
            start_trim(h)

        @pl.when(y + h < RING)
        def _():
            hop(2, 0, h, down).wait_recv()

        start_trim(3 + h)

    def absent(dy, core):
        if dy == 0:
            return jnp.bool_(False)
        if dy > 0:
            return y + dy >= RING
        if dy == -1 and core == 1:
            return jnp.bool_(False)
        return y + dy >= 0

    def pair(h):
        return pl.ds(2 * (h % 4), 2)

    def along(k, h):
        return remote(
            kv.at[k, c, pair(h)], kv.at[k + 1, c, pair(h)],
            x_send.at[k], x_recv.at[k + 1, h % 4], me + 2 * BLOCKS,
        )

    def cross(k, h, core):
        blocks = kv.at[k, core, pair(h)]
        return remote(blocks, blocks, c_send.at[k], c_recv.at[k, h % 4], twin)

    def from_x(k):
        return (k == 1) | ((k == 4) & (c == 0))

    def feeds_x(k):
        return ((k == 0) | ((k == 3) & (c == 0))) & (ring + 2 < RINGS)

    def launch(k):
        @pl.when(k == 2)
        def _():
            start_trim(0)
            start_trim(3)

        @pl.when(k != 2)
        def _():
            hop(k, 0, -1, up).start()
            hop(k, 0, 1, down).start()

    def edge_copy(to):
        return remote(kv.at[0, c, 0], edge, e_send, e_recv, to)

    def send_half():
        @pl.when(ring + 1 < RINGS)
        def _():
            xz(3, me + BLOCKS).start()

        @pl.when(gives_edge)
        def _():
            edge_copy(me + REACH * BLOCKS + 1).start()

    @pl.when(half == 1)
    def _():
        send_half()

    launch(0)

    @pl.when(ring + 4 < RINGS)
    def _():
        xz(2, me + 4 * BLOCKS).start()

    def arrive(k, h):
        @pl.when(from_x(k))
        def _():
            along(k - 1, h).wait_recv()

        @pl.when(k == 2)
        def _():
            arrive_trim(h)

        @pl.when(jnp.logical_not(from_x(k)) & (k != 2))
        def _():
            if h == 4:
                hop(k, 0, 4, up).wait_recv()
            else:
                for side, to, core in ((-1, up, 0), (1, down, 1)):
                    hop(k, 0, side * h, to).wait_recv()
                    if h < 3:
                        hop(k, side * h, side * (h + 1), to).start()
                    else:

                        @pl.when(c == core)
                        def _():
                            hop(k, side * 3, 4, to).start()

        cross(k, h, c).start()

        @pl.when(feeds_x(k))
        def _():
            along(k, h).start()

    lane = lax.broadcasted_iota(jnp.int32, (TOK, TOK), 1)
    row = lax.broadcasted_iota(jnp.int32, (TOK, TOK), 0)
    gap = row - lane

    def fold(blocks, ahead):
        keys = jnp.concatenate([b[pl.ds(0, TOK), :] for b in blocks], axis=0)
        values = jnp.concatenate([b[pl.ds(TOK, TOK), :] for b in blocks], axis=0)
        allowed = []
        for b, a in zip(blocks, ahead):
            seg = b[pl.ds(2 * TOK, 16), :].astype(jnp.float32)[0:1, :]
            allowed.append((seg == qseg[...]) & (gap >= a))
        score = lax.dot_general(
            q[...], keys, (((1,), (1,)), ((), ())), preferred_element_type=jnp.float32
        )
        rounded, keeps = [], []
        for h in range(HEADS):
            parts = [
                jnp.where(
                    allowed[n],
                    score[h * TOK : (h + 1) * TOK, n * TOK : (n + 1) * TOK] * unit_scale,
                    LOW,
                )
                for n in range(len(blocks))
            ]
            old = top[h]
            most = functools.reduce(jnp.maximum, parts)
            new = jnp.maximum(old, jnp.max(most, axis=1, keepdims=True))
            keep = jnp.exp2(old - new)
            weights = [jnp.exp2(p - new) for p in parts]
            top[h] = new
            total[h] = total[h] * keep + functools.reduce(jnp.add, weights)
            rounded.append(jnp.concatenate([w.astype(jnp.bfloat16) for w in weights], axis=1))
            keeps.append(keep)
        product = jnp.dot(
            jnp.concatenate(rounded, axis=0), values, preferred_element_type=jnp.float32
        )
        for h in range(HEADS):
            summed[h] = summed[h] * keeps[h] + product[h * TOK : (h + 1) * TOK]

    def unit(k, h):
        cross(k, h, 1 - c).wait_recv()
        blocks, ahead = [], []
        for dy in (0, 4) if h == 4 else (-h, h):
            for core in range(2):
                b = 2 * lax.rem(y + dy + RING, RING) + core
                blocks.append(kv.at[k, core, PLACE[dy]])
                a = (b - off - delta(k) * BLOCKS) * TOK
                ahead.append(jnp.where((k == 2) & absent(dy, core), TOK, a))
        fold(blocks, ahead)

    def drain(k):
        whole = kv.at[k, c]

        @pl.when(k == 2)
        def _():
            for go, copy in trims():

                @pl.when(go)
                def _():
                    copy().wait_send()

        @pl.when(jnp.logical_not(from_x(k)) & (k != 2))
        def _():
            sent = kv.at[k, c, pl.ds(0, 7)]
            remote(sent, sent, y_send.at[k], y_recv.at[k, 0], up).wait_send()

        @pl.when(feeds_x(k))
        def _():
            remote(whole, whole, x_send.at[k], x_recv.at[k, 0], twin).wait_send()

        remote(whole, whole, c_send.at[k], c_recv.at[k, 0], twin).wait_send()

    def pick(j):
        k = jnp.int32(-1)
        for n, (a, b) in enumerate(zip(LOW_STEPS, HIGH_STEPS)):
            k = jnp.where(j == a + (b - a) * half, n, k)
        return k

    def here(k):
        return (k >= 0) & (ring >= delta(jnp.maximum(k, 0)))

    def xy():
        return remote(
            kv.at[3, c, 0], kv.at[4, c, 0], xz_send.at[4], xz_recv.at[4], me + 2 * BLOCKS
        )

    hands_on = (c == 1) & (ring >= 1) & (ring + 2 < RINGS)

    def begin(k):
        @pl.when(here(k) & jnp.logical_not(from_x(k)))
        def _():
            xz(k, me).wait_recv()

            @pl.when((k == 3) & hands_on)
            def _():
                xy().start()

            launch(k)

    begin(jnp.int32(2))

    def step(j, _):
        @pl.when((half == 0) & (j == MEET))
        def _():
            pl.semaphore_wait(barrier, others)
            send_half()

        for h in (4, 3, 2, 1):
            now = pick(j - LAG * (h - 1))
            past = pick(j - LAG * (h - 1) - 2)

            @pl.when(here(now))
            def _():
                arrive(now, h)

            @pl.when(here(past))
            def _():
                unit(past, h)

        begin(pick(j + 2))
        done = pick(j - LAG * 3 - 1)

        @pl.when(here(done))
        def _():
            drain(done)

        @pl.when(has_edge & (j == LOW_STEPS[4] + LAG))
        def _():
            edge_copy(me).wait_recv()
            fold([edge], [jnp.int32(-ITEMS * BLOCKS * TOK + (BLOCKS - 1) * TOK)])

        return 0

    lax.fori_loop(0, max(LOW_STEPS[4], HIGH_STEPS[4]) + LAG * 3 + 3, step, 0)

    for h in range(HEADS):
        whole = jnp.sum(total[h], axis=1, keepdims=True)
        o_ref[:, h * HEAD : (h + 1) * HEAD] = (summed[h] * (1.0 / whole)).astype(jnp.bfloat16)

    for k in (2, 3):

        @pl.when(ring + BACK[k] < RINGS)
        def _():
            xz(k, me).wait_send()

    @pl.when(hands_on)
    def _():
        xy().wait_send()

    @pl.when(gives_edge)
    def _():
        edge_copy(me).wait_send()


def body(queries, keys, values, segment_ids):
    vmem = pl.BlockSpec(memory_space=pltpu.VMEM)
    return pl.pallas_call(
        kernel,
        out_shape=jax.ShapeDtypeStruct(queries.shape, queries.dtype),
        in_specs=[pl.BlockSpec(memory_space=pltpu.HBM)] * 4,
        out_specs=vmem,
        scratch_shapes=[
            pltpu.VMEM((HEADS * TOK, HEAD), jnp.bfloat16),
            pltpu.VMEM((1, TOK), jnp.int32),
            pltpu.VMEM((ITEMS, 2, RING, ROWS, HEAD), jnp.bfloat16),
            pltpu.VMEM((ROWS, HEAD), jnp.bfloat16),
            pltpu.VMEM((TOK, TOK), jnp.float32),
            pltpu.VMEM((HEADS, TOK, HEAD), jnp.float32),
            pltpu.VMEM((HEADS, TOK, HEAD), jnp.float32),
            pltpu.VMEM((HEADS, TOK, HEAD), jnp.float32),
            pltpu.SemaphoreType.DMA((3 + HEADS,)),
            pltpu.SemaphoreType.DMA((ITEMS,)),
            pltpu.SemaphoreType.DMA((ITEMS,)),
            pltpu.SemaphoreType.DMA((ITEMS,)),
            pltpu.SemaphoreType.DMA((ITEMS, RING)),
            pltpu.SemaphoreType.DMA((ITEMS,)),
            pltpu.SemaphoreType.DMA((ITEMS, 4)),
            pltpu.SemaphoreType.DMA((ITEMS,)),
            pltpu.SemaphoreType.DMA((ITEMS, 4)),
            pltpu.SemaphoreType.DMA((7,)),
            pltpu.SemaphoreType.DMA,
            pltpu.SemaphoreType.DMA,
        ],
        compiler_params=pltpu.CompilerParams(
            collective_id=0, has_side_effects=True, vmem_limit_bytes=60 << 20
        ),
        name="attend_ring",
    )(queries, keys, values, segment_ids.reshape(1, TOK))


def solution(mesh):
    return jax.shard_map(
        body,
        mesh=mesh,
        in_specs=(P("ctx", "kvh"), P("ctx", "kvh"), P("ctx", "kvh"), P("ctx")),
        out_specs=P("ctx", "kvh"),
        check_vma=False,
    )
```
